32 devices in a mesh: aux: 4 (over y, x), orb: 8 (over z, core).
Axes of the slice: x: 2, y: 2, z: 4, core: 2. Of those that a mesh axis runs over, the one named last changes fastest.
Arguments:
- integrals: bfloat16 [16, 15360, 2048], P(None, 'aux', 'orb'), may hold values from -6 to 6
- coeffs: bfloat16 [2048, 2048], P('orb'), may hold values from -1 to 1
- domains: int32 [16], replicated, may hold values from 0 to 15
- eps_occ: float32 [16], replicated, may hold values from -1.5 to -0.3
- eps_vir: float32 [2048], replicated, may hold values from 0.1 to 2.5
- pair_mask: int32 [16, 16], P('aux', 'orb'), may hold values 0 or 1
Outputs:
- amplitudes: bfloat16 [16, 128, 16, 128], P('aux', None, 'orb')
- energies: float32 [16, 16], P('aux', 'orb')
The draws below stay inside these ranges and needn't reach their ends.
Inputs may be any that keep to these rules, and one draw needn't show every extreme that they name: `domains`: each entry names one of the 16 virtual blocks.
All inputs are finite; a program needn't handle non-finite values. No bound on the sum of `pair_mask` on one device may be relied on, other than what follows from the above.
Results may differ from the reference program's by a relative error of at most 0.019.
Values may be sent and summed in bfloat16 or wider, within the bound.
A program may use at most 128 MiB of HBM per device.

```python
import jax
import jax.numpy as jnp
from jax import lax

NAUX = 15360
NAO = 2048
BS = 128
NVB = 16
NOCC = 16
N_ORB = 8


def draw_integrals(key, part):
    key = jax.random.fold_in(key, 11)
    shared_key, single_key = jax.random.split(key)
    shared = jnp.clip(jax.random.normal(shared_key, (NAUX, NAO), jnp.float32), -4.0, 4.0)
    single = jnp.clip(jax.random.normal(single_key, (NOCC, NAUX, NAO), jnp.float32), -4.0, 4.0)
    values = 0.7745967 * shared[None, :, :] + 0.6324555 * single
    return values.astype(jnp.bfloat16)


def draw_coeffs(key, part):
    key = jax.random.fold_in(key, 23)
    shared_key, single_key = jax.random.split(key)
    shared = jnp.clip(jax.random.normal(shared_key, (NAO, 1, BS), jnp.float32), -4.0, 4.0)
    single = jnp.clip(jax.random.normal(single_key, (NAO, NVB, BS), jnp.float32), -4.0, 4.0)
    scale = jnp.float32(NAO) ** (-0.5)
    values = (0.7416198 * shared + 0.6708204 * single) * scale
    return values.reshape(NAO, NVB * BS).astype(jnp.bfloat16)


def place_ends(values, key, low, top_value):
    longest = values.shape.index(max(values.shape))
    spots = []
    for shift in (0, 1):
        where = [jax.random.randint(jax.random.fold_in(key, axis), (), 0, length) for axis, length in enumerate(values.shape)]
        where[longest] = (where[longest] + shift) % values.shape[longest]
        spots.append(tuple(where))
    return values.at[spots[0]].set(low).at[spots[1]].set(top_value)


def setup_inputs(seed: int = 0) -> dict:
    key_list = jax.random.split(jax.random.key(seed), 7)
    return {
        "integrals": draw_integrals(jax.random.fold_in(key_list[6], 71), 0),
        "coeffs": draw_coeffs(jax.random.fold_in(key_list[6], 71), 0),
        "domains": place_ends(jax.random.randint(key_list[2], (NOCC,), 0, NVB), jax.random.fold_in(key_list[2], 1), 0, NVB - 1).astype(jnp.int32),
        "eps_occ": jnp.clip(jax.random.uniform(key_list[3], (NOCC,), jnp.float32, -1.5, -0.3), -1.5, -0.3),
        "eps_vir": jnp.clip(jax.random.uniform(key_list[4], (NVB * BS,), jnp.float32, 0.1, 2.5), 0.1, 2.5),
        "pair_mask": place_ends((jax.random.randint(key_list[5], (NOCC, NOCC), 0, 4) < 3).astype(jnp.int32), jax.random.fold_in(key_list[5], 1), 0, 1),
    }


def reference(integrals, coeffs, domains, eps_occ, eps_vir, pair_mask):
    vir_blocks = coeffs.reshape(NAO, NVB, BS)
    chosen = jnp.transpose(jnp.take(vir_blocks, domains, axis=1), (1, 0, 2))
    ao_local = NAO // N_ORB

    def add_group(orb_group, running):
        first = (orb_group * ao_local).astype(jnp.int32)
        part_ints = lax.dynamic_slice_in_dim(integrals, first, ao_local, 2).astype(jnp.float32)
        part_coef = lax.dynamic_slice_in_dim(chosen, first, ao_local, 1).astype(jnp.float32)
        partial_value = jnp.einsum('ipm,imb->ipb', part_ints, part_coef).astype(jnp.bfloat16)
        partial_value = lax.optimization_barrier(partial_value)
        return running + partial_value.astype(jnp.float32)
    running = jnp.zeros((NOCC, NAUX, BS), jnp.float32)
    running = lax.fori_loop(0, N_ORB, add_group, running)
    blocks = running.astype(jnp.bfloat16).astype(jnp.float32)
    pair_ints = jnp.einsum('jpb,ipa->jbia', blocks, blocks) * (1.0 / jnp.sqrt(jnp.float32(NAUX)))
    vir_energy = eps_vir.reshape(NVB, BS)[domains]
    denominator = vir_energy[:, :, None, None] + vir_energy[None, None, :, :] - eps_occ[:, None, None, None] - eps_occ[None, None, :, None]
    screen = pair_mask.astype(jnp.float32)
    amp = screen[:, None, :, None] * pair_ints / denominator
    energies = -lax.optimization_barrier(jnp.sum(pair_ints * amp, axis=(1, 3))) / float(BS * BS)
    return (amp.astype(jnp.bfloat16), energies)
```

```python
import functools

import jax
import jax.numpy as jnp
from jax import lax
from jax.experimental import pallas as pl
from jax.experimental.pallas import tpu as pltpu
from jax.sharding import PartitionSpec as P

NAUX = 15360
BS = 128
GROUP = 2 * BS
CHUNK_ROWS = 240
LEAD = 4
SLOTS = 4
IN_FLIGHT = 4
MESH = pl.DeviceIdType.MESH


def exchange(
    dims,
    coef_ref, x_ref, total_ref,
    xo, xp, zin, pin, psend, bt, gsend, grecv, gz, gfin,
    xo_sem, xp_sem, ps_sem, pr_sem, zs_sem, zr_sem, gs_sem, gr_sem, fs_sem, fr_sem,
):
    n_aux, n_orb, groups, per_group, row_groups = dims
    chips = n_orb // 2
    half = per_group * CHUNK_ROWS
    chunks = groups * per_group
    aux = lax.axis_index("aux")
    orb = lax.axis_index("orb")
    core = lax.rem(orb, 2)
    chip = orb // 2
    peer = chip * 2 + 1 - core
    stage = jnp.where(core == 0, chip, chips - 1 - chip)
    following = jnp.where(core == 0, lax.rem(orb + 2, n_orb), lax.rem(orb + n_orb - 2, n_orb))
    last = stage == chips - 1

    barrier = pltpu.get_barrier_semaphore()
    for d in range(1, n_orb):
        pl.semaphore_signal(barrier, inc=1, device_id=(aux, lax.rem(orb + d, n_orb)), device_id_type=MESH)
    for d in range(1, n_aux):
        pl.semaphore_signal(barrier, inc=1, device_id=(lax.rem(aux + d, n_aux), orb), device_id_type=MESH)
    pl.semaphore_wait(barrier, n_orb - 1 + n_aux - 1)

    def load(t, base, buf, sem):
        g, u = t // per_group, lax.rem(t, per_group)
        start = pl.multiple_of(base * half + u * CHUNK_ROWS, 16)
        slot = lax.rem(t, SLOTS)
        return pltpu.make_async_copy(
            x_ref.at[pl.ds(g * 2, 2), pl.ds(start, CHUNK_ROWS), :], buf.at[slot], sem.at[slot]
        )

    def load_own(t):
        return load(t, core, xo, xo_sem)

    def load_other(t):
        return load(t, 1 - core, xp, xp_sem)

    def transform(t, buf):
        g = t // per_group
        slot = lax.rem(t, SLOTS)
        parts = []
        for k in range(2):
            parts.append(
                jnp.dot(buf[slot, k], coef_ref[g * 2 + k], preferred_element_type=jnp.float32)
            )
        return jnp.concatenate(parts, axis=1)

    def to_peer(t):
        return pltpu.make_async_remote_copy(
            psend.at[t], pin.at[t], ps_sem.at[t], pr_sem.at[t], device_id=(aux, peer), device_id_type=MESH
        )

    def to_next(t):
        return pltpu.make_async_remote_copy(
            zin.at[t], zin.at[t], zs_sem.at[t], zr_sem.at[t], device_id=(aux, following), device_id_type=MESH
        )

    def to_row_owner(par, idx, r, col):
        owner = r // row_groups
        d = lax.rem(aux - owner + n_aux, n_aux)
        d = jnp.maximum(d, 1)
        rl = lax.rem(r, row_groups)
        return pltpu.make_async_remote_copy(
            gsend.at[par, idx], grecv.at[d - 1, rl, col], gs_sem.at[par, idx], gr_sem.at[d - 1, rl, col],
            device_id=(owner, orb), device_id_type=MESH,
        )

    def to_owner(rl, col):
        return pltpu.make_async_remote_copy(
            gz.at[rl, col], gfin.at[core, rl], fs_sem.at[rl, col], fr_sem.at[core, rl],
            device_id=(aux, col), device_id_type=MESH,
        )

    def each_block(g, fn):
        def body(r, carry):
            fn(r, r, g)

            @pl.when(r < g)
            def _():
                fn(groups + r, g, r)

            return carry

        lax.fori_loop(0, g + 1, body, 0)

    def drain(g):
        par = lax.rem(g, 2)

        def one(idx, r, col):
            @pl.when(r // row_groups != aux)
            def _():
                to_row_owner(par, idx, r, col).wait_send()

        each_block(g, one)

    def gram(g):
        par = lax.rem(g, 2)

        @pl.when(g >= 2)
        def _():
            drain(g - 2)

        first = g * per_group
        bt[g] = zin[pl.ds(first, per_group)].reshape(half, GROUP).T

        def send(idx, r, col):
            @pl.when(r // row_groups != aux)
            def _():
                to_row_owner(par, idx, r, col).start()

        def body(r, carry):
            block = jnp.dot(
                bt[r], zin[pl.ds(first, per_group)].reshape(half, GROUP), preferred_element_type=jnp.float32
            )
            gsend[par, r] = block.astype(jnp.bfloat16)
            send(r, r, g)

            @pl.when(r < g)
            def _():
                gsend[par, groups + r] = block.T.astype(jnp.bfloat16)
                send(groups + r, g, r)

            return carry

        lax.fori_loop(0, g + 1, body, 0)

    def combine(g):
        par = lax.rem(g, 2)

        def one(idx, r, col):
            @pl.when(r // row_groups == aux)
            def _():
                rl = lax.rem(r, row_groups)
                acc = gsend[par, idx].astype(jnp.float32)
                for d in range(1, n_aux):
                    pltpu.make_async_remote_copy(
                        gsend.at[par, idx], grecv.at[d - 1, rl, col], gs_sem.at[par, idx],
                        gr_sem.at[d - 1, rl, col], device_id=(aux, peer), device_id_type=MESH,
                    ).wait_recv()
                    acc += grecv[d - 1, rl, col].astype(jnp.float32)
                value = acc.astype(jnp.bfloat16)

                @pl.when(col == orb)
                def _():
                    gfin[core, rl] = value

                @pl.when(col != orb)
                def _():
                    gz[rl, col] = value
                    to_owner(rl, col).start()

        each_block(g, one)

    for t in range(SLOTS):
        load_other(t).start()
        load_own(t).start()

    def step(t, carry):
        @pl.when(t < chunks)
        def _():
            load_other(t).wait()
            psend[t] = transform(t, xp).astype(jnp.bfloat16)
            to_peer(t).start()

            @pl.when(t + SLOTS < chunks)
            def _():
                load_other(t + SLOTS).start()

        @pl.when(t >= LEAD)
        def _():
            now = t - LEAD
            load_own(now).wait()
            own = transform(now, xo)

            @pl.when(now + SLOTS < chunks)
            def _():
                load_own(now + SLOTS).start()

            to_peer(now).wait_recv()
            own += pin[now].astype(jnp.float32)

            @pl.when(stage == 0)
            def _():
                zin[now] = own.astype(jnp.bfloat16)

            @pl.when(stage > 0)
            def _():
                to_next(now).wait_recv()
                zin[now] = (own + zin[now].astype(jnp.float32)).astype(jnp.bfloat16)

            @pl.when(jnp.logical_not(last))
            def _():
                @pl.when(now >= IN_FLIGHT)
                def _():
                    to_next(now - IN_FLIGHT).wait_send()

                to_next(now).start()

            @pl.when(jnp.logical_and(last, lax.rem(now, per_group) == per_group - 1))
            def _():
                g = now // per_group
                gram(g)

                @pl.when(g >= 1)
                def _():
                    combine(g - 1)

        return carry

    lax.fori_loop(0, chunks + LEAD, step, 0)

    @pl.when(last)
    def _():
        combine(groups - 1)

    for end in range(2):
        finisher = 2 * (chips - 1) if end == 0 else 1
        for rl in range(row_groups):
            @pl.when(orb != finisher)
            def _():
                pltpu.make_async_remote_copy(
                    gz.at[rl, 0], gfin.at[end, rl], fs_sem.at[rl, 0], fr_sem.at[end, rl],
                    device_id=(aux, peer), device_id_type=MESH,
                ).wait_recv()

    for rl in range(row_groups):
        total_ref[rl] = gfin[0, rl].astype(jnp.float32) + gfin[1, rl].astype(jnp.float32)

    def sent(t, carry):
        to_peer(t).wait_send()
        return carry

    lax.fori_loop(0, chunks, sent, 0)

    @pl.when(jnp.logical_not(last))
    def _():
        for k in range(IN_FLIGHT):
            to_next(chunks - IN_FLIGHT + k).wait_send()

    @pl.when(last)
    def _():
        if groups >= 2:
            drain(groups - 2)
        drain(groups - 1)

        def left(col, carry):
            @pl.when(col != orb)
            def _():
                for rl in range(row_groups):
                    to_owner(rl, col).wait_send()

            return carry

        lax.fori_loop(0, groups, left, 0)


def pick(dom_ref, coef_ref, chosen_ref):
    for i in range(chosen_ref.shape[0]):
        first = pl.multiple_of(dom_ref[i] * BS, BS)
        chosen_ref[i] = coef_ref[:, pl.ds(first, BS)]


def pair_totals(integrals, coeffs, domains):
    n_aux, n_orb = lax.axis_size("aux"), lax.axis_size("orb")
    occupied, aux_rows, ao_local = integrals.shape
    groups = occupied // 2
    half = aux_rows // 2
    per_group = half // CHUNK_ROWS
    chunks = groups * per_group
    row_groups = occupied // n_aux // 2
    assert groups == n_orb and half % CHUNK_ROWS == 0
    dims = (n_aux, n_orb, groups, per_group, row_groups)
    bf16 = jnp.bfloat16
    chosen = pl.pallas_call(
        pick,
        out_shape=jax.ShapeDtypeStruct((occupied, ao_local, BS), bf16),
        in_specs=[pl.BlockSpec(memory_space=pltpu.SMEM), pl.BlockSpec(memory_space=pltpu.VMEM)],
        out_specs=pl.BlockSpec(memory_space=pltpu.VMEM),
    )(domains, coeffs)
    vmem = pltpu.VMEM
    dma = pltpu.SemaphoreType.DMA
    return pl.pallas_call(
        functools.partial(exchange, dims),
        out_shape=jax.ShapeDtypeStruct((row_groups, GROUP, GROUP), jnp.float32),
        in_specs=[
            pl.BlockSpec(memory_space=pltpu.VMEM),
            pl.BlockSpec(memory_space=pl.ANY),
        ],
        out_specs=pl.BlockSpec(memory_space=pltpu.VMEM),
        scratch_shapes=[
            vmem((SLOTS, 2, CHUNK_ROWS, ao_local), bf16),
            vmem((SLOTS, 2, CHUNK_ROWS, ao_local), bf16),
            vmem((chunks, CHUNK_ROWS, GROUP), bf16),
            vmem((chunks, CHUNK_ROWS, GROUP), bf16),
            vmem((chunks, CHUNK_ROWS, GROUP), bf16),
            vmem((groups, GROUP, half), bf16),
            vmem((2, 2 * groups, GROUP, GROUP), bf16),
            vmem((n_aux - 1, row_groups, groups, GROUP, GROUP), bf16),
            vmem((row_groups, groups, GROUP, GROUP), bf16),
            vmem((2, row_groups, GROUP, GROUP), bf16),
            dma((SLOTS,)),
            dma((SLOTS,)),
            dma((chunks,)),
            dma((chunks,)),
            dma((chunks,)),
            dma((chunks,)),
            dma((2, 2 * groups)),
            dma((n_aux - 1, row_groups, groups)),
            dma((row_groups, groups)),
            dma((2, row_groups)),
        ],
        compiler_params=pltpu.CompilerParams(
            collective_id=0, has_side_effects=True, vmem_limit_bytes=62 * 1024 * 1024
        ),
        cost_estimate=pl.CostEstimate(
            flops=2 * occupied * aux_rows * ao_local * BS, bytes_accessed=2 * integrals.size, transcendentals=0
        ),
    )(chosen, integrals)


def shards(integrals, coeffs, domains, eps_occ, eps_vir, pair_mask):
    occupied = integrals.shape[0]
    vir_blocks = coeffs.shape[1] // BS
    own_count = occupied // lax.axis_size("orb")
    row_count = occupied // lax.axis_size("aux")
    aux_index = lax.axis_index("aux")
    orb_index = lax.axis_index("orb")
    totals = pair_totals(integrals, coeffs, domains).reshape(row_count, BS, own_count, BS)
    pair_ints = totals * (1.0 / jnp.sqrt(jnp.float32(NAUX)))
    selector = domains[:, None] == jnp.arange(vir_blocks, dtype=jnp.int32)[None, :]
    vir_energy = jnp.dot(
        selector.astype(jnp.float32),
        eps_vir.reshape(vir_blocks, BS),
        precision=lax.Precision.HIGHEST,
    )
    vir_rows = lax.dynamic_slice_in_dim(vir_energy, aux_index * row_count, row_count, 0)
    vir_cols = lax.dynamic_slice_in_dim(vir_energy, orb_index * own_count, own_count, 0)
    occ_rows = lax.dynamic_slice_in_dim(eps_occ, aux_index * row_count, row_count, 0)
    occ_cols = lax.dynamic_slice_in_dim(eps_occ, orb_index * own_count, own_count, 0)
    denominator = (
        vir_rows[:, :, None, None]
        + vir_cols[None, None, :, :]
        - occ_rows[:, None, None, None]
        - occ_cols[None, None, :, None]
    )
    screen = pair_mask.astype(jnp.float32)
    amplitudes = screen[:, None, :, None] * pair_ints / denominator
    energies = -jnp.sum(pair_ints * amplitudes, axis=(1, 3)) / float(BS * BS)
    return (amplitudes.astype(jnp.bfloat16), energies)


def solution(mesh):
    return jax.shard_map(
        shards,
        mesh=mesh,
        in_specs=(P(None, "aux", "orb"), P("orb", None), P(), P(), P(), P("aux", "orb")),
        out_specs=(P("aux", None, "orb", None), P("aux", "orb")),
        check_vma=False,
    )
```

```python
import functools

import jax
import jax.numpy as jnp
from jax import lax
from jax.experimental import pallas as pl
from jax.experimental.pallas import tpu as pltpu
from jax.sharding import PartitionSpec as P

NAUX = 15360
BS = 128
GROUP = 2 * BS
CHUNK_ROWS = 240
LEAD = 6
SLOTS = 4
OTHER_SLOTS = 8
IN_FLIGHT = 4
MESH = pl.DeviceIdType.MESH


def exchange(
    dims,
    coef_ref, x_ref, total_ref,
    xo, xp, zin, pin, psend, bt, gsend, grecv, gz, gfin,
    xo_sem, xp_sem, ps_sem, pr_sem, zs_sem, zr_sem, gs_sem, gr_sem, fs_sem, fr_sem,
):
    n_aux, n_orb, groups, per_group, row_groups = dims
    chips = n_orb // 2
    half = per_group * CHUNK_ROWS
    chunks = groups * per_group
    aux = lax.axis_index("aux")
    orb = lax.axis_index("orb")
    core = lax.rem(orb, 2)
    chip = orb // 2
    peer = chip * 2 + 1 - core
    stage = jnp.where(core == 0, chip, chips - 1 - chip)
    following = jnp.where(core == 0, lax.rem(orb + 2, n_orb), lax.rem(orb + n_orb - 2, n_orb))
    last = stage == chips - 1

    barrier = pltpu.get_barrier_semaphore()
    for d in range(1, n_orb):
        pl.semaphore_signal(barrier, inc=1, device_id=(aux, lax.rem(orb + d, n_orb)), device_id_type=MESH)
    for d in range(1, n_aux):
        pl.semaphore_signal(barrier, inc=1, device_id=(lax.rem(aux + d, n_aux), orb), device_id_type=MESH)
    pl.semaphore_wait(barrier, n_orb - 1 + n_aux - 1)

    def load(t, base, buf, sem, slots):
        g, u = t // per_group, lax.rem(t, per_group)
        start = pl.multiple_of(base * half + u * CHUNK_ROWS, 16)
        slot = lax.rem(t, slots)
        return pltpu.make_async_copy(
            x_ref.at[pl.ds(g * 2, 2), pl.ds(start, CHUNK_ROWS), :], buf.at[slot], sem.at[slot]
        )

    def load_own(t):
        return load(t, core, xo, xo_sem, SLOTS)

    def load_other(t):
        return load(t, 1 - core, xp, xp_sem, OTHER_SLOTS)

    def transform(t, buf, slots):
        g = t // per_group
        slot = lax.rem(t, slots)
        parts = []
        for k in range(2):
            parts.append(
                jnp.dot(buf[slot, k], coef_ref[g * 2 + k], preferred_element_type=jnp.float32)
            )
        return jnp.concatenate(parts, axis=1)

    def to_peer(t):
        return pltpu.make_async_remote_copy(
            psend.at[t], pin.at[t], ps_sem.at[t], pr_sem.at[t], device_id=(aux, peer), device_id_type=MESH
        )

    def to_next(t):
        return pltpu.make_async_remote_copy(
            zin.at[t], zin.at[t], zs_sem.at[t], zr_sem.at[t], device_id=(aux, following), device_id_type=MESH
        )

    def to_row_owner(par, idx, r, col):
        owner = r // row_groups
        d = lax.rem(aux - owner + n_aux, n_aux)
        d = jnp.maximum(d, 1)
        rl = lax.rem(r, row_groups)
        return pltpu.make_async_remote_copy(
            gsend.at[par, idx], grecv.at[d - 1, rl, col], gs_sem.at[par, idx], gr_sem.at[d - 1, rl, col],
            device_id=(owner, orb), device_id_type=MESH,
        )

    def to_owner(rl, col):
        return pltpu.make_async_remote_copy(
            gz.at[rl, col], gfin.at[core, rl], fs_sem.at[rl, col], fr_sem.at[core, rl],
            device_id=(aux, col), device_id_type=MESH,
        )

    def each_block(g, fn):
        def body(r, carry):
            fn(r, r, g)

            @pl.when(r < g)
            def _():
                fn(groups + r, g, r)

            return carry

        lax.fori_loop(0, g + 1, body, 0)

    def drain(g):
        par = lax.rem(g, 2)

        def one(idx, r, col):
            @pl.when(r // row_groups != aux)
            def _():
                to_row_owner(par, idx, r, col).wait_send()

        each_block(g, one)

    def gram(g):
        par = lax.rem(g, 2)

        @pl.when(g >= 2)
        def _():
            drain(g - 2)

        first = g * per_group

        def send(idx, r, col):
            @pl.when(r // row_groups != aux)
            def _():
                to_row_owner(par, idx, r, col).start()

        def column():
            return zin[pl.ds(first, per_group)].reshape(half, GROUP)

        def body(r, carry):
            block = jnp.dot(bt[r], column(), preferred_element_type=jnp.float32)
            gsend[par, r] = block.astype(jnp.bfloat16)
            send(r, r, g)
            gsend[par, groups + r] = block.T.astype(jnp.bfloat16)
            send(groups + r, g, r)
            return carry

        lax.fori_loop(0, g, body, 0)
        bt[g] = column().T
        gsend[par, g] = jnp.dot(bt[g], column(), preferred_element_type=jnp.float32).astype(jnp.bfloat16)
        send(g, g, g)

    def combine(g):
        par = lax.rem(g, 2)

        def one(idx, r, col):
            @pl.when(r // row_groups == aux)
            def _():
                rl = lax.rem(r, row_groups)
                acc = gsend[par, idx].astype(jnp.float32)
                for d in range(1, n_aux):
                    pltpu.make_async_remote_copy(
                        gsend.at[par, idx], grecv.at[d - 1, rl, col], gs_sem.at[par, idx],
                        gr_sem.at[d - 1, rl, col], device_id=(aux, peer), device_id_type=MESH,
                    ).wait_recv()
                    acc += grecv[d - 1, rl, col].astype(jnp.float32)
                value = acc.astype(jnp.bfloat16)

                @pl.when(col == orb)
                def _():
                    gfin[core, rl] = value

                @pl.when(col != orb)
                def _():
                    gz[rl, col] = value
                    to_owner(rl, col).start()

        each_block(g, one)

    for t in range(OTHER_SLOTS):
        load_other(t).start()
    for t in range(SLOTS):
        load_own(t).start()

    def help_peer(t):
        load_other(t).wait()
        psend[t] = transform(t, xp, OTHER_SLOTS).astype(jnp.bfloat16)
        to_peer(t).start()

        @pl.when(t + OTHER_SLOTS < chunks)
        def _():
            load_other(t + OTHER_SLOTS).start()

    def ahead(t, carry):
        help_peer(t)
        return carry

    lax.fori_loop(0, LEAD, ahead, 0)

    def step(now, carry):
        for k in range(2):
            t = LEAD + 2 * now + k

            @pl.when(t < chunks)
            def _():
                help_peer(t)

        load_own(now).wait()
        own = transform(now, xo, SLOTS)

        @pl.when(now + SLOTS < chunks)
        def _():
            load_own(now + SLOTS).start()

        to_peer(now).wait_recv()
        own += pin[now].astype(jnp.float32)

        @pl.when(stage == 0)
        def _():
            zin[now] = own.astype(jnp.bfloat16)

        @pl.when(stage > 0)
        def _():
            to_next(now).wait_recv()
            zin[now] = (own + zin[now].astype(jnp.float32)).astype(jnp.bfloat16)

        @pl.when(jnp.logical_not(last))
        def _():
            @pl.when(now >= IN_FLIGHT)
            def _():
                to_next(now - IN_FLIGHT).wait_send()

            to_next(now).start()

        @pl.when(jnp.logical_and(last, lax.rem(now, per_group) == per_group - 1))
        def _():
            g = now // per_group
            gram(g)

            @pl.when(g >= 1)
            def _():
                combine(g - 1)

        return carry

    lax.fori_loop(0, chunks, step, 0)

    @pl.when(last)
    def _():
        combine(groups - 1)

    for end in range(2):
        finisher = 2 * (chips - 1) if end == 0 else 1
        for rl in range(row_groups):
            @pl.when(orb != finisher)
            def _():
                pltpu.make_async_remote_copy(
                    gz.at[rl, 0], gfin.at[end, rl], fs_sem.at[rl, 0], fr_sem.at[end, rl],
                    device_id=(aux, peer), device_id_type=MESH,
                ).wait_recv()

    for rl in range(row_groups):
        total_ref[rl] = gfin[0, rl].astype(jnp.float32) + gfin[1, rl].astype(jnp.float32)

    def sent(t, carry):
        to_peer(t).wait_send()
        return carry

    lax.fori_loop(0, chunks, sent, 0)

    @pl.when(jnp.logical_not(last))
    def _():
        for k in range(IN_FLIGHT):
            to_next(chunks - IN_FLIGHT + k).wait_send()

    @pl.when(last)
    def _():
        if groups >= 2:
            drain(groups - 2)
        drain(groups - 1)

        def left(col, carry):
            @pl.when(col != orb)
            def _():
                for rl in range(row_groups):
                    to_owner(rl, col).wait_send()

            return carry

        lax.fori_loop(0, groups, left, 0)


def pick(dom_ref, coef_ref, chosen_ref):
    for i in range(chosen_ref.shape[0]):
        first = pl.multiple_of(dom_ref[i] * BS, BS)
        chosen_ref[i] = coef_ref[:, pl.ds(first, BS)]


def pair_totals(integrals, coeffs, domains):
    n_aux, n_orb = lax.axis_size("aux"), lax.axis_size("orb")
    occupied, aux_rows, ao_local = integrals.shape
    groups = occupied // 2
    half = aux_rows // 2
    per_group = half // CHUNK_ROWS
    chunks = groups * per_group
    row_groups = occupied // n_aux // 2
    assert groups == n_orb and half % CHUNK_ROWS == 0
    dims = (n_aux, n_orb, groups, per_group, row_groups)
    bf16 = jnp.bfloat16
    chosen = pl.pallas_call(
        pick,
        out_shape=jax.ShapeDtypeStruct((occupied, ao_local, BS), bf16),
        in_specs=[pl.BlockSpec(memory_space=pltpu.SMEM), pl.BlockSpec(memory_space=pltpu.VMEM)],
        out_specs=pl.BlockSpec(memory_space=pltpu.VMEM),
    )(domains, coeffs)
    vmem = pltpu.VMEM
    dma = pltpu.SemaphoreType.DMA
    return pl.pallas_call(
        functools.partial(exchange, dims),
        out_shape=jax.ShapeDtypeStruct((row_groups, GROUP, GROUP), jnp.float32),
        in_specs=[
            pl.BlockSpec(memory_space=pltpu.VMEM),
            pl.BlockSpec(memory_space=pl.ANY),
        ],
        out_specs=pl.BlockSpec(memory_space=pltpu.VMEM),
        scratch_shapes=[
            vmem((SLOTS, 2, CHUNK_ROWS, ao_local), bf16),
            vmem((OTHER_SLOTS, 2, CHUNK_ROWS, ao_local), bf16),
            vmem((chunks, CHUNK_ROWS, GROUP), bf16),
            vmem((chunks, CHUNK_ROWS, GROUP), bf16),
            vmem((chunks, CHUNK_ROWS, GROUP), bf16),
            vmem((groups, GROUP, half), bf16),
            vmem((2, 2 * groups, GROUP, GROUP), bf16),
            vmem((n_aux - 1, row_groups, groups, GROUP, GROUP), bf16),
            vmem((row_groups, groups, GROUP, GROUP), bf16),
            vmem((2, row_groups, GROUP, GROUP), bf16),
            dma((SLOTS,)),
            dma((OTHER_SLOTS,)),
            dma((chunks,)),
            dma((chunks,)),
            dma((chunks,)),
            dma((chunks,)),
            dma((2, 2 * groups)),
            dma((n_aux - 1, row_groups, groups)),
            dma((row_groups, groups)),
            dma((2, row_groups)),
        ],
        compiler_params=pltpu.CompilerParams(
            collective_id=0, has_side_effects=True, vmem_limit_bytes=62 * 1024 * 1024
        ),
        cost_estimate=pl.CostEstimate(
            flops=2 * occupied * aux_rows * ao_local * BS, bytes_accessed=2 * integrals.size, transcendentals=0
        ),
    )(chosen, integrals)


def shards(integrals, coeffs, domains, eps_occ, eps_vir, pair_mask):
    occupied = integrals.shape[0]
    vir_blocks = coeffs.shape[1] // BS
    own_count = occupied // lax.axis_size("orb")
    row_count = occupied // lax.axis_size("aux")
    aux_index = lax.axis_index("aux")
    orb_index = lax.axis_index("orb")
    totals = pair_totals(integrals, coeffs, domains).reshape(row_count, BS, own_count, BS)
    pair_ints = totals * (1.0 / jnp.sqrt(jnp.float32(NAUX)))
    selector = domains[:, None] == jnp.arange(vir_blocks, dtype=jnp.int32)[None, :]
    vir_energy = jnp.dot(
        selector.astype(jnp.float32),
        eps_vir.reshape(vir_blocks, BS),
        precision=lax.Precision.HIGHEST,
    )
    vir_rows = lax.dynamic_slice_in_dim(vir_energy, aux_index * row_count, row_count, 0)
    vir_cols = lax.dynamic_slice_in_dim(vir_energy, orb_index * own_count, own_count, 0)
    occ_rows = lax.dynamic_slice_in_dim(eps_occ, aux_index * row_count, row_count, 0)
    occ_cols = lax.dynamic_slice_in_dim(eps_occ, orb_index * own_count, own_count, 0)
    denominator = (
        vir_rows[:, :, None, None]
        + vir_cols[None, None, :, :]
        - occ_rows[:, None, None, None]
        - occ_cols[None, None, :, None]
    )
    screen = pair_mask.astype(jnp.float32)
    amplitudes = screen[:, None, :, None] * pair_ints / denominator
    energies = -jnp.sum(pair_ints * amplitudes, axis=(1, 3)) / float(BS * BS)
    return (amplitudes.astype(jnp.bfloat16), energies)


def solution(mesh):
    return jax.shard_map(
        shards,
        mesh=mesh,
        in_specs=(P(None, "aux", "orb"), P("orb", None), P(), P(), P(), P("aux", "orb")),
        out_specs=(P("aux", None, "orb", None), P("aux", "orb")),
        check_vma=False,
    )
```

```python
import functools

import jax
import jax.numpy as jnp
from jax import lax
from jax.experimental import pallas as pl
from jax.experimental.pallas import tpu as pltpu
from jax.sharding import PartitionSpec as P

NAUX = 15360
BS = 128
GROUP = 2 * BS
CHUNK_ROWS = 240
LEAD = 6
SLOTS = 4
OTHER_SLOTS = 8
IN_FLIGHT = 4
MESH = pl.DeviceIdType.MESH


def exchange(
    dims,
    coef_ref, x_ref, total_ref,
    xo, xp, zin, pin, psend, bt, gsend, grecv, gz, gzt, gfin, gin, ffin,
    xo_sem, xp_sem, ps_sem, pr_sem, zs_sem, zr_sem, gs_sem, gr_sem, fs_sem, fr_sem, ts_sem, tr_sem, ws_sem, wr_sem,
):
    n_aux, n_orb, groups, per_group, row_groups = dims
    chips = n_orb // 2
    half = per_group * CHUNK_ROWS
    chunks = groups * per_group
    aux = lax.axis_index("aux")
    orb = lax.axis_index("orb")
    core = lax.rem(orb, 2)
    chip = orb // 2
    peer = chip * 2 + 1 - core
    stage = jnp.where(core == 0, chip, chips - 1 - chip)
    following = jnp.where(core == 0, lax.rem(orb + 2, n_orb), lax.rem(orb + n_orb - 2, n_orb))
    last = stage == chips - 1

    barrier = pltpu.get_barrier_semaphore()
    for d in range(1, n_orb):
        pl.semaphore_signal(barrier, inc=1, device_id=(aux, lax.rem(orb + d, n_orb)), device_id_type=MESH)
    for d in range(1, n_aux):
        pl.semaphore_signal(barrier, inc=1, device_id=(lax.rem(aux + d, n_aux), orb), device_id_type=MESH)
    pl.semaphore_wait(barrier, n_orb - 1 + n_aux - 1)

    def load(t, base, buf, sem, slots):
        g, u = t // per_group, lax.rem(t, per_group)
        start = pl.multiple_of(base * half + u * CHUNK_ROWS, 16)
        slot = lax.rem(t, slots)
        return pltpu.make_async_copy(
            x_ref.at[pl.ds(g * 2, 2), pl.ds(start, CHUNK_ROWS), :], buf.at[slot], sem.at[slot]
        )

    def load_own(t):
        return load(t, core, xo, xo_sem, SLOTS)

    def load_other(t):
        return load(t, 1 - core, xp, xp_sem, OTHER_SLOTS)

    def transform(t, buf, slots):
        g = t // per_group
        slot = lax.rem(t, slots)
        parts = []
        for k in range(2):
            parts.append(
                jnp.dot(buf[slot, k], coef_ref[g * 2 + k], preferred_element_type=jnp.float32)
            )
        return jnp.concatenate(parts, axis=1)

    def to_peer(t):
        return pltpu.make_async_remote_copy(
            psend.at[t], pin.at[t], ps_sem.at[t], pr_sem.at[t], device_id=(aux, peer), device_id_type=MESH
        )

    def to_next(t):
        return pltpu.make_async_remote_copy(
            zin.at[t], zin.at[t], zs_sem.at[t], zr_sem.at[t], device_id=(aux, following), device_id_type=MESH
        )

    def line_of(r):
        return r // row_groups

    def native(a, b):
        lo, hi = jnp.minimum(a, b), jnp.maximum(a, b)
        takes_hi = jnp.logical_and(hi != groups - 1, lax.rem(lo, 2) == 1)
        return jnp.where(takes_hi, hi, lo)

    def to_reducer(par, r, g):
        n = native(r, g)
        m = r + g - n
        owner = line_of(n)
        d = jnp.maximum(lax.rem(aux - owner + n_aux, n_aux), 1)
        rl = lax.rem(n, row_groups)
        return pltpu.make_async_remote_copy(
            gsend.at[par, r], grecv.at[d - 1, rl, m], gs_sem.at[par, r], gr_sem.at[d - 1, rl, m],
            device_id=(owner, orb), device_id_type=MESH,
        )

    def to_owner(rl, m):
        return pltpu.make_async_remote_copy(
            gz.at[rl, m], gfin.at[core, rl], fs_sem.at[rl, m], fr_sem.at[core, rl],
            device_id=(aux, m), device_id_type=MESH,
        )

    def to_forwarder(rl, m, n):
        return pltpu.make_async_remote_copy(
            gzt.at[rl, m], gin.at[core, m], ts_sem.at[rl, m], tr_sem.at[core, m],
            device_id=(aux, n), device_id_type=MESH,
        )

    def forward(m):
        return pltpu.make_async_remote_copy(
            gin.at[0, m], ffin.at[lax.rem(m, row_groups)], ws_sem.at[m], wr_sem.at[lax.rem(m, row_groups)],
            device_id=(line_of(m), orb), device_id_type=MESH,
        )

    def drain(g):
        par = lax.rem(g, 2)

        def body(r, carry):
            @pl.when(line_of(native(r, g)) != aux)
            def _():
                to_reducer(par, r, g).wait_send()

            return carry

        lax.fori_loop(0, g + 1, body, 0)

    def gram(g):
        par = lax.rem(g, 2)

        @pl.when(g >= 2)
        def _():
            drain(g - 2)

        first = g * per_group

        def column():
            return zin[pl.ds(first, per_group)].reshape(half, GROUP)

        def block(r):
            gsend[par, r] = jnp.dot(bt[r], column(), preferred_element_type=jnp.float32).astype(jnp.bfloat16)

            @pl.when(line_of(native(r, g)) != aux)
            def _():
                to_reducer(par, r, g).start()

        def body(r, carry):
            block(r)
            return carry

        lax.fori_loop(0, g, body, 0)
        bt[g] = column().T
        block(g)

    def combine(g):
        par = lax.rem(g, 2)

        def body(r, carry):
            n = native(r, g)
            m = r + g - n
            rl = lax.rem(n, row_groups)

            @pl.when(line_of(n) == aux)
            def _():
                acc = gsend[par, r].astype(jnp.float32)
                for d in range(1, n_aux):
                    pltpu.make_async_remote_copy(
                        gsend.at[par, r], grecv.at[d - 1, rl, m], gs_sem.at[par, r], gr_sem.at[d - 1, rl, m],
                        device_id=(aux, peer), device_id_type=MESH,
                    ).wait_recv()
                    acc += grecv[d - 1, rl, m].astype(jnp.float32)

                def deliver(straight, turned):
                    @pl.when(m == orb)
                    def _():
                        gfin[core, rl] = straight().astype(jnp.bfloat16)

                    @pl.when(m != orb)
                    def _():
                        gz[rl, m] = straight().astype(jnp.bfloat16)
                        to_owner(rl, m).start()

                    @pl.when(m != n)
                    def _():
                        @pl.when(n == orb)
                        def _():
                            gin[core, m] = turned().astype(jnp.bfloat16)

                        @pl.when(n != orb)
                        def _():
                            gzt[rl, m] = turned().astype(jnp.bfloat16)
                            to_forwarder(rl, m, n).start()

                @pl.when(n == r)
                def _():
                    deliver(lambda: acc, lambda: acc.T)

                @pl.when(n != r)
                def _():
                    deliver(lambda: acc.T, lambda: acc)

            return carry

        lax.fori_loop(0, g + 1, body, 0)

    for t in range(OTHER_SLOTS):
        load_other(t).start()
    for t in range(SLOTS):
        load_own(t).start()

    def help_peer(t):
        load_other(t).wait()
        psend[t] = transform(t, xp, OTHER_SLOTS).astype(jnp.bfloat16)
        to_peer(t).start()

        @pl.when(t + OTHER_SLOTS < chunks)
        def _():
            load_other(t + OTHER_SLOTS).start()

    def ahead(t, carry):
        help_peer(t)
        return carry

    lax.fori_loop(0, LEAD, ahead, 0)

    def step(now, carry):
        for k in range(2):
            t = LEAD + 2 * now + k

            @pl.when(t < chunks)
            def _():
                help_peer(t)

        load_own(now).wait()
        own = transform(now, xo, SLOTS)

        @pl.when(now + SLOTS < chunks)
        def _():
            load_own(now + SLOTS).start()

        to_peer(now).wait_recv()
        own += pin[now].astype(jnp.float32)

        @pl.when(stage == 0)
        def _():
            zin[now] = own.astype(jnp.bfloat16)

        @pl.when(stage > 0)
        def _():
            to_next(now).wait_recv()
            zin[now] = (own + zin[now].astype(jnp.float32)).astype(jnp.bfloat16)

        @pl.when(jnp.logical_not(last))
        def _():
            @pl.when(now >= IN_FLIGHT)
            def _():
                to_next(now - IN_FLIGHT).wait_send()

            to_next(now).start()

        g = now // per_group

        @pl.when(jnp.logical_and(jnp.logical_and(last, g >= 1), lax.rem(now, per_group) == per_group // 2))
        def _():
            combine(g - 1)

        @pl.when(jnp.logical_and(last, lax.rem(now, per_group) == per_group - 1))
        def _():
            gram(g)

        return carry

    lax.fori_loop(0, chunks, step, 0)

    @pl.when(last)
    def _():
        combine(groups - 1)

    finishers = (2 * (chips - 1), 1)

    def pass_on(m, carry):
        @pl.when(jnp.logical_and(m != orb, native(orb, m) == orb))
        def _():
            for end in range(2):
                @pl.when(orb != finishers[end])
                def _():
                    pltpu.make_async_remote_copy(
                        gzt.at[0, 0], gin.at[end, m], ts_sem.at[0, 0], tr_sem.at[end, m],
                        device_id=(aux, peer), device_id_type=MESH,
                    ).wait_recv()

            both = gin[0, m].astype(jnp.float32) + gin[1, m].astype(jnp.float32)

            @pl.when(line_of(m) == aux)
            def _():
                total_ref[lax.rem(m, row_groups)] = both

            @pl.when(line_of(m) != aux)
            def _():
                gin[0, m] = both.astype(jnp.bfloat16)
                forward(m).start()

        return carry

    @pl.when(line_of(orb) == aux)
    def _():
        lax.fori_loop(0, groups, pass_on, 0)

    for rl in range(row_groups):
        r = aux * row_groups + rl

        @pl.when(native(r, orb) == r)
        def _():
            for end in range(2):
                @pl.when(orb != finishers[end])
                def _():
                    pltpu.make_async_remote_copy(
                        gz.at[rl, 0], gfin.at[end, rl], fs_sem.at[rl, 0], fr_sem.at[end, rl],
                        device_id=(aux, peer), device_id_type=MESH,
                    ).wait_recv()

            total_ref[rl] = gfin[0, rl].astype(jnp.float32) + gfin[1, rl].astype(jnp.float32)

        @pl.when(jnp.logical_and(native(r, orb) != r, line_of(orb) != aux))
        def _():
            pltpu.make_async_remote_copy(
                gin.at[0, 0], ffin.at[rl], ws_sem.at[0], wr_sem.at[rl],
                device_id=(aux, peer), device_id_type=MESH,
            ).wait_recv()
            total_ref[rl] = ffin[rl].astype(jnp.float32)

    def sent(t, carry):
        to_peer(t).wait_send()
        return carry

    lax.fori_loop(0, chunks, sent, 0)

    @pl.when(jnp.logical_not(last))
    def _():
        for k in range(IN_FLIGHT):
            to_next(chunks - IN_FLIGHT + k).wait_send()

    @pl.when(last)
    def _():
        if groups >= 2:
            drain(groups - 2)
        drain(groups - 1)

        def left(m, carry):
            for rl in range(row_groups):
                n = aux * row_groups + rl

                @pl.when(native(n, m) == n)
                def _():
                    @pl.when(m != orb)
                    def _():
                        to_owner(rl, m).wait_send()

                    @pl.when(jnp.logical_and(m != n, n != orb))
                    def _():
                        to_forwarder(rl, m, n).wait_send()

            return carry

        lax.fori_loop(0, groups, left, 0)

    @pl.when(line_of(orb) == aux)
    def _():
        def passed(m, carry):
            @pl.when(jnp.logical_and(native(orb, m) == orb, line_of(m) != aux))
            def _():
                forward(m).wait_send()

            return carry

        lax.fori_loop(0, groups, passed, 0)


def pick(dom_ref, coef_ref, chosen_ref):
    for i in range(chosen_ref.shape[0]):
        first = pl.multiple_of(dom_ref[i] * BS, BS)
        chosen_ref[i] = coef_ref[:, pl.ds(first, BS)]


def pair_totals(integrals, coeffs, domains):
    n_aux, n_orb = lax.axis_size("aux"), lax.axis_size("orb")
    occupied, aux_rows, ao_local = integrals.shape
    groups = occupied // 2
    half = aux_rows // 2
    per_group = half // CHUNK_ROWS
    chunks = groups * per_group
    row_groups = occupied // n_aux // 2
    assert groups == n_orb and half % CHUNK_ROWS == 0
    dims = (n_aux, n_orb, groups, per_group, row_groups)
    bf16 = jnp.bfloat16
    chosen = pl.pallas_call(
        pick,
        out_shape=jax.ShapeDtypeStruct((occupied, ao_local, BS), bf16),
        in_specs=[pl.BlockSpec(memory_space=pltpu.SMEM), pl.BlockSpec(memory_space=pltpu.VMEM)],
        out_specs=pl.BlockSpec(memory_space=pltpu.VMEM),
    )(domains, coeffs)
    vmem = pltpu.VMEM
    dma = pltpu.SemaphoreType.DMA
    return pl.pallas_call(
        functools.partial(exchange, dims),
        out_shape=jax.ShapeDtypeStruct((row_groups, GROUP, GROUP), jnp.float32),
        in_specs=[
            pl.BlockSpec(memory_space=pltpu.VMEM),
            pl.BlockSpec(memory_space=pl.ANY),
        ],
        out_specs=pl.BlockSpec(memory_space=pltpu.VMEM),
        scratch_shapes=[
            vmem((SLOTS, 2, CHUNK_ROWS, ao_local), bf16),
            vmem((OTHER_SLOTS, 2, CHUNK_ROWS, ao_local), bf16),
            vmem((chunks, CHUNK_ROWS, GROUP), bf16),
            vmem((chunks, CHUNK_ROWS, GROUP), bf16),
            vmem((chunks, CHUNK_ROWS, GROUP), bf16),
            vmem((groups, GROUP, half), bf16),
            vmem((2, groups, GROUP, GROUP), bf16),
            vmem((n_aux - 1, row_groups, groups, GROUP, GROUP), bf16),
            vmem((row_groups, groups, GROUP, GROUP), bf16),
            vmem((row_groups, groups, GROUP, GROUP), bf16),
            vmem((2, row_groups, GROUP, GROUP), bf16),
            vmem((2, groups, GROUP, GROUP), bf16),
            vmem((row_groups, GROUP, GROUP), bf16),
            dma((SLOTS,)),
            dma((OTHER_SLOTS,)),
            dma((chunks,)),
            dma((chunks,)),
            dma((chunks,)),
            dma((chunks,)),
            dma((2, groups)),
            dma((n_aux - 1, row_groups, groups)),
            dma((row_groups, groups)),
            dma((2, row_groups)),
            dma((row_groups, groups)),
            dma((2, groups)),
            dma((groups,)),
            dma((row_groups,)),
        ],
        compiler_params=pltpu.CompilerParams(
            collective_id=0, has_side_effects=True, vmem_limit_bytes=62 * 1024 * 1024
        ),
        cost_estimate=pl.CostEstimate(
            flops=2 * occupied * aux_rows * ao_local * BS, bytes_accessed=2 * integrals.size, transcendentals=0
        ),
    )(chosen, integrals)


def shards(integrals, coeffs, domains, eps_occ, eps_vir, pair_mask):
    occupied = integrals.shape[0]
    vir_blocks = coeffs.shape[1] // BS
    own_count = occupied // lax.axis_size("orb")
    row_count = occupied // lax.axis_size("aux")
    aux_index = lax.axis_index("aux")
    orb_index = lax.axis_index("orb")
    totals = pair_totals(integrals, coeffs, domains).reshape(row_count, BS, own_count, BS)
    pair_ints = totals * (1.0 / jnp.sqrt(jnp.float32(NAUX)))
    selector = domains[:, None] == jnp.arange(vir_blocks, dtype=jnp.int32)[None, :]
    vir_energy = jnp.dot(
        selector.astype(jnp.float32),
        eps_vir.reshape(vir_blocks, BS),
        precision=lax.Precision.HIGHEST,
    )
    vir_rows = lax.dynamic_slice_in_dim(vir_energy, aux_index * row_count, row_count, 0)
    vir_cols = lax.dynamic_slice_in_dim(vir_energy, orb_index * own_count, own_count, 0)
    occ_rows = lax.dynamic_slice_in_dim(eps_occ, aux_index * row_count, row_count, 0)
    occ_cols = lax.dynamic_slice_in_dim(eps_occ, orb_index * own_count, own_count, 0)
    denominator = (
        vir_rows[:, :, None, None]
        + vir_cols[None, None, :, :]
        - occ_rows[:, None, None, None]
        - occ_cols[None, None, :, None]
    )
    screen = pair_mask.astype(jnp.float32)
    amplitudes = screen[:, None, :, None] * pair_ints / denominator
    energies = -jnp.sum(pair_ints * amplitudes, axis=(1, 3)) / float(BS * BS)
    return (amplitudes.astype(jnp.bfloat16), energies)


def solution(mesh):
    return jax.shard_map(
        shards,
        mesh=mesh,
        in_specs=(P(None, "aux", "orb"), P("orb", None), P(), P(), P(), P("aux", "orb")),
        out_specs=(P("aux", None, "orb", None), P("aux", "orb")),
        check_vma=False,
    )
```

```python
import functools

import jax
import jax.numpy as jnp
from jax import lax
from jax.experimental import pallas as pl
from jax.experimental.pallas import tpu as pltpu
from jax.sharding import PartitionSpec as P

NAUX = 15360
BS = 128
GROUP = 2 * BS
CHUNK_ROWS = 240
LEAD = 6
SLOTS = 4
OTHER_SLOTS = 8
SEND_SLOTS = 16
IN_FLIGHT = 4
MESH = pl.DeviceIdType.MESH


def exchange(
    dims,
    dom_ref, coef_hbm, x_ref, total_ref,
    coef_ref, gacc, xo, xp, zin, pin, psend, bt, gsend, grecv, gz, gzt, gfin, gin, ffin,
    coef_sem, xo_sem, xp_sem, ps_sem, pr_sem, zs_sem, zr_sem, gs_sem, gr_sem, fs_sem, fr_sem, ts_sem, tr_sem, ws_sem, wr_sem,
):
    n_aux, n_orb, groups, per_group, row_groups, parts = dims
    part_chunks = per_group // parts
    send_slots = psend.shape[0]
    chips = n_orb // 2
    half = per_group * CHUNK_ROWS
    chunks = groups * per_group
    aux = lax.axis_index("aux")
    orb = lax.axis_index("orb")
    core = lax.rem(orb, 2)
    chip = orb // 2
    peer = chip * 2 + 1 - core
    stage = jnp.where(core == 0, chip, chips - 1 - chip)
    following = jnp.where(core == 0, lax.rem(orb + 2, n_orb), lax.rem(orb + n_orb - 2, n_orb))
    last = stage == chips - 1

    def load(t, base, buf, sem, slots):
        g, u = t // per_group, lax.rem(t, per_group)
        start = pl.multiple_of(base * half + u * CHUNK_ROWS, 16)
        slot = lax.rem(t, slots)
        return pltpu.make_async_copy(
            x_ref.at[pl.ds(g * 2, 2), pl.ds(start, CHUNK_ROWS), :], buf.at[slot], sem.at[slot]
        )

    def load_own(t):
        return load(t, core, xo, xo_sem, SLOTS)

    def load_other(t):
        return load(t, 1 - core, xp, xp_sem, OTHER_SLOTS)

    def transform(t, buf, slots):
        g = t // per_group
        slot = lax.rem(t, slots)
        parts = []
        for k in range(2):
            parts.append(
                jnp.dot(buf[slot, k], coef_ref[dom_ref[g * 2 + k]], preferred_element_type=jnp.float32)
            )
        return jnp.concatenate(parts, axis=1)

    def to_peer(t):
        return pltpu.make_async_remote_copy(
            psend.at[lax.rem(t, send_slots)], pin.at[t], ps_sem.at[lax.rem(t, send_slots)], pr_sem.at[t], device_id=(aux, peer), device_id_type=MESH
        )

    def to_next(t):
        return pltpu.make_async_remote_copy(
            zin.at[t], zin.at[t], zs_sem.at[t], zr_sem.at[t], device_id=(aux, following), device_id_type=MESH
        )

    def line_of(r):
        return r // row_groups

    def native(a, b):
        lo, hi = jnp.minimum(a, b), jnp.maximum(a, b)
        takes_hi = jnp.logical_and(hi != groups - 1, lax.rem(lo, 2) == 1)
        return jnp.where(takes_hi, hi, lo)

    def to_reducer(par, r, g):
        n = native(r, g)
        m = r + g - n
        owner = line_of(n)
        d = jnp.maximum(lax.rem(aux - owner + n_aux, n_aux), 1)
        rl = lax.rem(n, row_groups)
        return pltpu.make_async_remote_copy(
            gsend.at[par, r], grecv.at[d - 1, rl, m], gs_sem.at[par, r], gr_sem.at[d - 1, rl, m],
            device_id=(owner, orb), device_id_type=MESH,
        )

    def to_owner(rl, m):
        return pltpu.make_async_remote_copy(
            gz.at[rl, m], gfin.at[core, rl], fs_sem.at[rl, m], fr_sem.at[core, rl],
            device_id=(aux, m), device_id_type=MESH,
        )

    def to_forwarder(rl, m, n):
        return pltpu.make_async_remote_copy(
            gzt.at[rl, m], gin.at[core, m], ts_sem.at[rl, m], tr_sem.at[core, m],
            device_id=(aux, n), device_id_type=MESH,
        )

    def forward(m):
        return pltpu.make_async_remote_copy(
            gin.at[0, m], ffin.at[lax.rem(m, row_groups)], ws_sem.at[m], wr_sem.at[lax.rem(m, row_groups)],
            device_id=(line_of(m), orb), device_id_type=MESH,
        )

    def drain(g):
        par = lax.rem(g, 2)

        def body(r, carry):
            @pl.when(line_of(native(r, g)) != aux)
            def _():
                to_reducer(par, r, g).wait_send()

            return carry

        lax.fori_loop(0, g + 1, body, 0)

    def gram(g, p):
        par = lax.rem(g, 2)

        @pl.when(jnp.logical_and(p == 0, g >= 2))
        def _():
            drain(g - 2)

        first = g * per_group + p * part_chunks

        def column():
            return zin[pl.ds(first, part_chunks)].reshape(part_chunks * CHUNK_ROWS, GROUP)

        def block(r):
            value = jnp.dot(bt[r, p], column(), preferred_element_type=jnp.float32)

            @pl.when(p == 0)
            def _():
                gacc[r] = value

            @pl.when(p > 0)
            def _():
                gacc[r] += value

            @pl.when(p == parts - 1)
            def _():
                gsend[par, r] = gacc[r].astype(jnp.bfloat16)

                @pl.when(line_of(native(r, g)) != aux)
                def _():
                    to_reducer(par, r, g).start()

        def body(r, carry):
            block(r)
            return carry

        lax.fori_loop(0, g, body, 0)
        bt[g, p] = column().T
        block(g)

    def combine(g):
        par = lax.rem(g, 2)

        def body(r, carry):
            n = native(r, g)
            m = r + g - n
            rl = lax.rem(n, row_groups)

            @pl.when(line_of(n) == aux)
            def _():
                acc = gsend[par, r].astype(jnp.float32)
                for d in range(1, n_aux):
                    pltpu.make_async_remote_copy(
                        gsend.at[par, r], grecv.at[d - 1, rl, m], gs_sem.at[par, r], gr_sem.at[d - 1, rl, m],
                        device_id=(aux, peer), device_id_type=MESH,
                    ).wait_recv()
                    acc += grecv[d - 1, rl, m].astype(jnp.float32)

                def deliver(straight, turned):
                    @pl.when(m == orb)
                    def _():
                        gfin[core, rl] = straight().astype(jnp.bfloat16)

                    @pl.when(m != orb)
                    def _():
                        gz[rl, m] = straight().astype(jnp.bfloat16)
                        to_owner(rl, m).start()

                    @pl.when(m != n)
                    def _():
                        @pl.when(n == orb)
                        def _():
                            gin[core, m] = turned().astype(jnp.bfloat16)

                        @pl.when(n != orb)
                        def _():
                            gzt[rl, m] = turned().astype(jnp.bfloat16)
                            to_forwarder(rl, m, n).start()

                @pl.when(n == r)
                def _():
                    deliver(lambda: acc, lambda: acc.T)

                @pl.when(n != r)
                def _():
                    deliver(lambda: acc.T, lambda: acc)

            return carry

        lax.fori_loop(0, g + 1, body, 0)

    coef_loads = [
        pltpu.make_async_copy(coef_hbm.at[:, pl.ds(v * BS, BS)], coef_ref.at[v], coef_sem.at[v])
        for v in range(coef_ref.shape[0])
    ]
    for copy in coef_loads:
        copy.start()
    for t in range(OTHER_SLOTS):
        load_other(t).start()
    for t in range(SLOTS):
        load_own(t).start()

    barrier = pltpu.get_barrier_semaphore()
    for d in range(1, n_orb):
        pl.semaphore_signal(barrier, inc=1, device_id=(aux, lax.rem(orb + d, n_orb)), device_id_type=MESH)
    for d in range(1, n_aux):
        pl.semaphore_signal(barrier, inc=1, device_id=(lax.rem(aux + d, n_aux), orb), device_id_type=MESH)
    pl.semaphore_wait(barrier, n_orb - 1 + n_aux - 1)

    for copy in coef_loads:
        copy.wait()

    def help_peer(t):
        load_other(t).wait()

        @pl.when(t >= send_slots)
        def _():
            to_peer(t - send_slots).wait_send()

        psend[lax.rem(t, send_slots)] = transform(t, xp, OTHER_SLOTS).astype(jnp.bfloat16)
        to_peer(t).start()

        @pl.when(t + OTHER_SLOTS < chunks)
        def _():
            load_other(t + OTHER_SLOTS).start()

    def ahead(t, carry):
        help_peer(t)
        return carry

    lax.fori_loop(0, LEAD, ahead, 0)

    def step(now, carry):
        for k in range(2):
            t = LEAD + 2 * now + k

            @pl.when(t < chunks)
            def _():
                help_peer(t)

        load_own(now).wait()
        own = transform(now, xo, SLOTS)

        @pl.when(now + SLOTS < chunks)
        def _():
            load_own(now + SLOTS).start()

        to_peer(now).wait_recv()
        own += pin[now].astype(jnp.float32)

        @pl.when(stage == 0)
        def _():
            zin[now] = own.astype(jnp.bfloat16)

        @pl.when(stage > 0)
        def _():
            to_next(now).wait_recv()
            zin[now] = (own + zin[now].astype(jnp.float32)).astype(jnp.bfloat16)

        @pl.when(jnp.logical_not(last))
        def _():
            @pl.when(now >= IN_FLIGHT)
            def _():
                to_next(now - IN_FLIGHT).wait_send()

            to_next(now).start()

        g = now // per_group

        @pl.when(jnp.logical_and(jnp.logical_and(last, g >= 1), lax.rem(now, per_group) == per_group // 2))
        def _():
            combine(g - 1)

        @pl.when(jnp.logical_and(last, lax.rem(now, part_chunks) == part_chunks - 1))
        def _():
            gram(g, lax.rem(now, per_group) // part_chunks)

        return carry

    lax.fori_loop(0, chunks, step, 0)

    @pl.when(last)
    def _():
        combine(groups - 1)

    finishers = (2 * (chips - 1), 1)

    def pass_on(m, carry):
        @pl.when(jnp.logical_and(m != orb, native(orb, m) == orb))
        def _():
            for end in range(2):
                @pl.when(orb != finishers[end])
                def _():
                    pltpu.make_async_remote_copy(
                        gzt.at[0, 0], gin.at[end, m], ts_sem.at[0, 0], tr_sem.at[end, m],
                        device_id=(aux, peer), device_id_type=MESH,
                    ).wait_recv()

            both = gin[0, m].astype(jnp.float32) + gin[1, m].astype(jnp.float32)

            @pl.when(line_of(m) == aux)
            def _():
                total_ref[lax.rem(m, row_groups)] = both

            @pl.when(line_of(m) != aux)
            def _():
                gin[0, m] = both.astype(jnp.bfloat16)
                forward(m).start()

        return carry

    @pl.when(line_of(orb) == aux)
    def _():
        lax.fori_loop(0, groups, pass_on, 0)

    for rl in range(row_groups):
        r = aux * row_groups + rl

        @pl.when(native(r, orb) == r)
        def _():
            for end in range(2):
                @pl.when(orb != finishers[end])
                def _():
                    pltpu.make_async_remote_copy(
                        gz.at[rl, 0], gfin.at[end, rl], fs_sem.at[rl, 0], fr_sem.at[end, rl],
                        device_id=(aux, peer), device_id_type=MESH,
                    ).wait_recv()

            total_ref[rl] = gfin[0, rl].astype(jnp.float32) + gfin[1, rl].astype(jnp.float32)

        @pl.when(jnp.logical_and(native(r, orb) != r, line_of(orb) != aux))
        def _():
            pltpu.make_async_remote_copy(
                gin.at[0, 0], ffin.at[rl], ws_sem.at[0], wr_sem.at[rl],
                device_id=(aux, peer), device_id_type=MESH,
            ).wait_recv()
            total_ref[rl] = ffin[rl].astype(jnp.float32)

    def sent(t, carry):
        to_peer(t).wait_send()
        return carry

    lax.fori_loop(chunks - send_slots, chunks, sent, 0)

    @pl.when(jnp.logical_not(last))
    def _():
        for k in range(IN_FLIGHT):
            to_next(chunks - IN_FLIGHT + k).wait_send()

    @pl.when(last)
    def _():
        if groups >= 2:
            drain(groups - 2)
        drain(groups - 1)

        def left(m, carry):
            for rl in range(row_groups):
                n = aux * row_groups + rl

                @pl.when(native(n, m) == n)
                def _():
                    @pl.when(m != orb)
                    def _():
                        to_owner(rl, m).wait_send()

                    @pl.when(jnp.logical_and(m != n, n != orb))
                    def _():
                        to_forwarder(rl, m, n).wait_send()

            return carry

        lax.fori_loop(0, groups, left, 0)

    @pl.when(line_of(orb) == aux)
    def _():
        def passed(m, carry):
            @pl.when(jnp.logical_and(native(orb, m) == orb, line_of(m) != aux))
            def _():
                forward(m).wait_send()

            return carry

        lax.fori_loop(0, groups, passed, 0)


def pair_totals(integrals, coeffs, domains):
    n_aux, n_orb = lax.axis_size("aux"), lax.axis_size("orb")
    occupied, aux_rows, ao_local = integrals.shape
    groups = occupied // 2
    half = aux_rows // 2
    per_group = half // CHUNK_ROWS
    chunks = groups * per_group
    row_groups = occupied // n_aux // 2
    assert groups == n_orb and half % CHUNK_ROWS == 0
    parts = next(n for n in (4, 2, 1) if per_group % n == 0)
    vir_blocks = coeffs.shape[1] // BS
    dims = (n_aux, n_orb, groups, per_group, row_groups, parts)
    bf16 = jnp.bfloat16
    vmem = pltpu.VMEM
    dma = pltpu.SemaphoreType.DMA
    return pl.pallas_call(
        functools.partial(exchange, dims),
        out_shape=jax.ShapeDtypeStruct((row_groups, GROUP, GROUP), jnp.float32),
        in_specs=[
            pl.BlockSpec(memory_space=pltpu.SMEM),
            pl.BlockSpec(memory_space=pl.ANY),
            pl.BlockSpec(memory_space=pl.ANY),
        ],
        out_specs=pl.BlockSpec(memory_space=pltpu.VMEM),
        scratch_shapes=[
            vmem((vir_blocks, ao_local, BS), bf16),
            vmem((groups, GROUP, GROUP), jnp.float32),
            vmem((SLOTS, 2, CHUNK_ROWS, ao_local), bf16),
            vmem((OTHER_SLOTS, 2, CHUNK_ROWS, ao_local), bf16),
            vmem((chunks, CHUNK_ROWS, GROUP), bf16),
            vmem((chunks, CHUNK_ROWS, GROUP), bf16),
            vmem((min(SEND_SLOTS, chunks), CHUNK_ROWS, GROUP), bf16),
            vmem((groups, parts, GROUP, half // parts), bf16),
            vmem((2, groups, GROUP, GROUP), bf16),
            vmem((n_aux - 1, row_groups, groups, GROUP, GROUP), bf16),
            vmem((row_groups, groups, GROUP, GROUP), bf16),
            vmem((row_groups, groups, GROUP, GROUP), bf16),
            vmem((2, row_groups, GROUP, GROUP), bf16),
            vmem((2, groups, GROUP, GROUP), bf16),
            vmem((row_groups, GROUP, GROUP), bf16),
            dma((vir_blocks,)),
            dma((SLOTS,)),
            dma((OTHER_SLOTS,)),
            dma((min(SEND_SLOTS, chunks),)),
            dma((chunks,)),
            dma((chunks,)),
            dma((chunks,)),
            dma((2, groups)),
            dma((n_aux - 1, row_groups, groups)),
            dma((row_groups, groups)),
            dma((2, row_groups)),
            dma((row_groups, groups)),
            dma((2, groups)),
            dma((groups,)),
            dma((row_groups,)),
        ],
        compiler_params=pltpu.CompilerParams(
            collective_id=0, has_side_effects=True, vmem_limit_bytes=63 * 1024 * 1024
        ),
        cost_estimate=pl.CostEstimate(
            flops=2 * occupied * aux_rows * ao_local * BS, bytes_accessed=2 * integrals.size, transcendentals=0
        ),
    )(domains, coeffs, integrals)


def shards(integrals, coeffs, domains, eps_occ, eps_vir, pair_mask):
    occupied = integrals.shape[0]
    vir_blocks = coeffs.shape[1] // BS
    own_count = occupied // lax.axis_size("orb")
    row_count = occupied // lax.axis_size("aux")
    aux_index = lax.axis_index("aux")
    orb_index = lax.axis_index("orb")
    totals = pair_totals(integrals, coeffs, domains).reshape(row_count, BS, own_count, BS)
    pair_ints = totals * (1.0 / jnp.sqrt(jnp.float32(NAUX)))
    selector = domains[:, None] == jnp.arange(vir_blocks, dtype=jnp.int32)[None, :]
    vir_energy = jnp.dot(
        selector.astype(jnp.float32),
        eps_vir.reshape(vir_blocks, BS),
        precision=lax.Precision.HIGHEST,
    )
    vir_rows = lax.dynamic_slice_in_dim(vir_energy, aux_index * row_count, row_count, 0)
    vir_cols = lax.dynamic_slice_in_dim(vir_energy, orb_index * own_count, own_count, 0)
    occ_rows = lax.dynamic_slice_in_dim(eps_occ, aux_index * row_count, row_count, 0)
    occ_cols = lax.dynamic_slice_in_dim(eps_occ, orb_index * own_count, own_count, 0)
    denominator = (
        vir_rows[:, :, None, None]
        + vir_cols[None, None, :, :]
        - occ_rows[:, None, None, None]
        - occ_cols[None, None, :, None]
    )
    screen = pair_mask.astype(jnp.float32)
    amplitudes = screen[:, None, :, None] * pair_ints / denominator
    energies = -jnp.sum(pair_ints * amplitudes, axis=(1, 3)) / float(BS * BS)
    return (amplitudes.astype(jnp.bfloat16), energies)


def solution(mesh):
    return jax.shard_map(
        shards,
        mesh=mesh,
        in_specs=(P(None, "aux", "orb"), P("orb", None), P(), P(), P(), P("aux", "orb")),
        out_specs=(P("aux", None, "orb", None), P("aux", "orb")),
        check_vma=False,
    )
```

```python
import functools

import jax
import jax.numpy as jnp
from jax import lax
from jax.experimental import pallas as pl
from jax.experimental.pallas import tpu as pltpu
from jax.sharding import PartitionSpec as P

NAUX = 15360
BS = 128
GROUP = 2 * BS
CHUNK_ROWS = 240
LEAD = 6
SLOTS = 4
OTHER_SLOTS = 8
SEND_SLOTS = 16
IN_FLIGHT = 4
MESH = pl.DeviceIdType.MESH


def exchange(
    dims,
    dom_ref, coef_hbm, x_ref, total_ref,
    coef_ref, gacc, xo, xp, zin, pin, psend, bt, gsend, grecv, gz, gzt, gfin, gin, ffin,
    coef_sem, xo_sem, xp_sem, ps_sem, pr_sem, zs_sem, zr_sem, gs_sem, gr_sem, fs_sem, fr_sem, ts_sem, tr_sem, ws_sem, wr_sem,
):
    n_aux, n_orb, groups, per_group, row_groups, parts = dims
    part_chunks = per_group // parts
    send_slots = psend.shape[0]
    chips = n_orb // 2
    half = per_group * CHUNK_ROWS
    chunks = groups * per_group
    aux = lax.axis_index("aux")
    orb = lax.axis_index("orb")
    core = lax.rem(orb, 2)
    chip = orb // 2
    peer = chip * 2 + 1 - core
    stage = jnp.where(core == 0, chip, chips - 1 - chip)
    following = jnp.where(core == 0, lax.rem(orb + 2, n_orb), lax.rem(orb + n_orb - 2, n_orb))
    last = stage == chips - 1

    def load(t, base, buf, sem, slots):
        g, u = t // per_group, lax.rem(t, per_group)
        start = pl.multiple_of(base * half + u * CHUNK_ROWS, 16)
        slot = lax.rem(t, slots)
        return pltpu.make_async_copy(
            x_ref.at[pl.ds(g * 2, 2), pl.ds(start, CHUNK_ROWS), :], buf.at[slot], sem.at[slot]
        )

    def load_own(t):
        return load(t, core, xo, xo_sem, SLOTS)

    def load_other(t):
        return load(t, 1 - core, xp, xp_sem, OTHER_SLOTS)

    def transform(t, buf, slots):
        g = t // per_group
        slot = lax.rem(t, slots)
        parts = []
        for k in range(2):
            parts.append(
                jnp.dot(buf[slot, k], coef_ref[dom_ref[g * 2 + k]], preferred_element_type=jnp.float32)
            )
        return jnp.concatenate(parts, axis=1)

    def to_peer(t):
        return pltpu.make_async_remote_copy(
            psend.at[lax.rem(t, send_slots)], pin.at[t], ps_sem.at[lax.rem(t, send_slots)], pr_sem.at[t], device_id=(aux, peer), device_id_type=MESH
        )

    def to_next(t):
        return pltpu.make_async_remote_copy(
            zin.at[t], zin.at[t], zs_sem.at[t], zr_sem.at[t], device_id=(aux, following), device_id_type=MESH
        )

    def line_of(r):
        return r // row_groups

    def native(a, b):
        lo, hi = jnp.minimum(a, b), jnp.maximum(a, b)
        takes_hi = jnp.logical_and(hi != groups - 1, lax.rem(lo, 2) == 1)
        return jnp.where(takes_hi, hi, lo)

    def to_reducer(par, r, g):
        n = native(r, g)
        m = r + g - n
        owner = line_of(n)
        d = jnp.maximum(lax.rem(aux - owner + n_aux, n_aux), 1)
        rl = lax.rem(n, row_groups)
        return pltpu.make_async_remote_copy(
            gsend.at[par, r], grecv.at[d - 1, rl, m], gs_sem.at[par, r], gr_sem.at[d - 1, rl, m],
            device_id=(owner, orb), device_id_type=MESH,
        )

    def to_owner(rl, m):
        return pltpu.make_async_remote_copy(
            gz.at[rl, m], gfin.at[core, rl], fs_sem.at[rl, m], fr_sem.at[core, rl],
            device_id=(aux, m), device_id_type=MESH,
        )

    def to_forwarder(rl, m, n):
        return pltpu.make_async_remote_copy(
            gzt.at[rl, m], gin.at[core, m], ts_sem.at[rl, m], tr_sem.at[core, m],
            device_id=(aux, n), device_id_type=MESH,
        )

    def forward(m):
        return pltpu.make_async_remote_copy(
            gin.at[0, m], ffin.at[lax.rem(m, row_groups)], ws_sem.at[m], wr_sem.at[lax.rem(m, row_groups)],
            device_id=(line_of(m), orb), device_id_type=MESH,
        )

    def drain(g):
        par = lax.rem(g, 2)

        def body(r, carry):
            @pl.when(line_of(native(r, g)) != aux)
            def _():
                to_reducer(par, r, g).wait_send()

            return carry

        lax.fori_loop(0, g + 1, body, 0)

    def gram(g, p):
        par = lax.rem(g, 2)

        @pl.when(jnp.logical_and(p == 0, g >= 2))
        def _():
            drain(g - 2)

        first = g * per_group + p * part_chunks

        def column():
            return zin[pl.ds(first, part_chunks)].reshape(part_chunks * CHUNK_ROWS, GROUP)

        def block(r):
            value = jnp.dot(bt[r, p], column(), preferred_element_type=jnp.float32)

            @pl.when(p == 0)
            def _():
                gacc[r] = value

            @pl.when(p > 0)
            def _():
                gacc[r] += value

            @pl.when(p == parts - 1)
            def _():
                gsend[par, r] = gacc[r].astype(jnp.bfloat16)

                @pl.when(line_of(native(r, g)) != aux)
                def _():
                    to_reducer(par, r, g).start()

        def body(r, carry):
            block(r)
            return carry

        lax.fori_loop(0, g, body, 0)
        bt[g, p] = column().T
        block(g)

    def combine(g):
        par = lax.rem(g, 2)

        def body(r, carry):
            n = native(r, g)
            m = r + g - n
            rl = lax.rem(n, row_groups)

            @pl.when(line_of(n) == aux)
            def _():
                acc = gsend[par, r].astype(jnp.float32)
                for d in range(1, n_aux):
                    pltpu.make_async_remote_copy(
                        gsend.at[par, r], grecv.at[d - 1, rl, m], gs_sem.at[par, r], gr_sem.at[d - 1, rl, m],
                        device_id=(aux, peer), device_id_type=MESH,
                    ).wait_recv()
                    acc += grecv[d - 1, rl, m].astype(jnp.float32)

                def deliver(straight, turned):
                    @pl.when(m != n)
                    def _():
                        @pl.when(n == orb)
                        def _():
                            gin[core, m] = turned().astype(jnp.bfloat16)

                        @pl.when(n != orb)
                        def _():
                            gzt[rl, m] = turned().astype(jnp.bfloat16)
                            to_forwarder(rl, m, n).start()

                    @pl.when(m == orb)
                    def _():
                        gfin[core, rl] = straight().astype(jnp.bfloat16)

                    @pl.when(m != orb)
                    def _():
                        gz[rl, m] = straight().astype(jnp.bfloat16)
                        to_owner(rl, m).start()

                @pl.when(n == r)
                def _():
                    deliver(lambda: acc, lambda: acc.T)

                @pl.when(n != r)
                def _():
                    deliver(lambda: acc.T, lambda: acc)

            return carry

        lax.fori_loop(0, g + 1, body, 0)

    coef_loads = [
        pltpu.make_async_copy(coef_hbm.at[:, pl.ds(v * BS, BS)], coef_ref.at[v], coef_sem.at[v])
        for v in range(coef_ref.shape[0])
    ]
    for copy in coef_loads:
        copy.start()
    for t in range(OTHER_SLOTS):
        load_other(t).start()
    for t in range(SLOTS):
        load_own(t).start()

    barrier = pltpu.get_barrier_semaphore()
    for d in range(1, n_orb):
        pl.semaphore_signal(barrier, inc=1, device_id=(aux, lax.rem(orb + d, n_orb)), device_id_type=MESH)
    for d in range(1, n_aux):
        pl.semaphore_signal(barrier, inc=1, device_id=(lax.rem(aux + d, n_aux), orb), device_id_type=MESH)
    pl.semaphore_wait(barrier, n_orb - 1 + n_aux - 1)

    for copy in coef_loads:
        copy.wait()

    def help_peer(t):
        load_other(t).wait()

        @pl.when(t >= send_slots)
        def _():
            to_peer(t - send_slots).wait_send()

        psend[lax.rem(t, send_slots)] = transform(t, xp, OTHER_SLOTS).astype(jnp.bfloat16)
        to_peer(t).start()

        @pl.when(t + OTHER_SLOTS < chunks)
        def _():
            load_other(t + OTHER_SLOTS).start()

    def ahead(t, carry):
        help_peer(t)
        return carry

    lax.fori_loop(0, LEAD, ahead, 0)

    def step(now, carry):
        for k in range(2):
            t = LEAD + 2 * now + k

            @pl.when(t < chunks)
            def _():
                help_peer(t)

        load_own(now).wait()
        own = transform(now, xo, SLOTS)

        @pl.when(now + SLOTS < chunks)
        def _():
            load_own(now + SLOTS).start()

        to_peer(now).wait_recv()
        own += pin[now].astype(jnp.float32)

        @pl.when(stage == 0)
        def _():
            zin[now] = own.astype(jnp.bfloat16)

        @pl.when(stage > 0)
        def _():
            to_next(now).wait_recv()
            zin[now] = (own + zin[now].astype(jnp.float32)).astype(jnp.bfloat16)

        @pl.when(jnp.logical_not(last))
        def _():
            @pl.when(now >= IN_FLIGHT)
            def _():
                to_next(now - IN_FLIGHT).wait_send()

            to_next(now).start()

        g = now // per_group

        @pl.when(jnp.logical_and(jnp.logical_and(last, g >= 1), lax.rem(now, per_group) == per_group // 2))
        def _():
            combine(g - 1)

        @pl.when(jnp.logical_and(last, lax.rem(now, part_chunks) == part_chunks - 1))
        def _():
            gram(g, lax.rem(now, per_group) // part_chunks)

        return carry

    lax.fori_loop(0, chunks, step, 0)

    @pl.when(last)
    def _():
        combine(groups - 1)

    finishers = (2 * (chips - 1), 1)

    def pass_on(m, carry):
        @pl.when(jnp.logical_and(m != orb, native(orb, m) == orb))
        def _():
            for end in range(2):
                @pl.when(orb != finishers[end])
                def _():
                    pltpu.make_async_remote_copy(
                        gzt.at[0, 0], gin.at[end, m], ts_sem.at[0, 0], tr_sem.at[end, m],
                        device_id=(aux, peer), device_id_type=MESH,
                    ).wait_recv()

            both = gin[0, m].astype(jnp.float32) + gin[1, m].astype(jnp.float32)

            @pl.when(line_of(m) == aux)
            def _():
                total_ref[lax.rem(m, row_groups)] = both

            @pl.when(line_of(m) != aux)
            def _():
                gin[0, m] = both.astype(jnp.bfloat16)
                forward(m).start()

        return carry

    @pl.when(line_of(orb) == aux)
    def _():
        lax.fori_loop(0, groups, pass_on, 0)

    for rl in range(row_groups):
        r = aux * row_groups + rl

        @pl.when(native(r, orb) == r)
        def _():
            for end in range(2):
                @pl.when(orb != finishers[end])
                def _():
                    pltpu.make_async_remote_copy(
                        gz.at[rl, 0], gfin.at[end, rl], fs_sem.at[rl, 0], fr_sem.at[end, rl],
                        device_id=(aux, peer), device_id_type=MESH,
                    ).wait_recv()

            total_ref[rl] = gfin[0, rl].astype(jnp.float32) + gfin[1, rl].astype(jnp.float32)

        @pl.when(jnp.logical_and(native(r, orb) != r, line_of(orb) != aux))
        def _():
            pltpu.make_async_remote_copy(
                gin.at[0, 0], ffin.at[rl], ws_sem.at[0], wr_sem.at[rl],
                device_id=(aux, peer), device_id_type=MESH,
            ).wait_recv()
            total_ref[rl] = ffin[rl].astype(jnp.float32)

    def sent(t, carry):
        to_peer(t).wait_send()
        return carry

    lax.fori_loop(chunks - send_slots, chunks, sent, 0)

    @pl.when(jnp.logical_not(last))
    def _():
        for k in range(IN_FLIGHT):
            to_next(chunks - IN_FLIGHT + k).wait_send()

    @pl.when(last)
    def _():
        if groups >= 2:
            drain(groups - 2)
        drain(groups - 1)

        def left(m, carry):
            for rl in range(row_groups):
                n = aux * row_groups + rl

                @pl.when(native(n, m) == n)
                def _():
                    @pl.when(m != orb)
                    def _():
                        to_owner(rl, m).wait_send()

                    @pl.when(jnp.logical_and(m != n, n != orb))
                    def _():
                        to_forwarder(rl, m, n).wait_send()

            return carry

        lax.fori_loop(0, groups, left, 0)

    @pl.when(line_of(orb) == aux)
    def _():
        def passed(m, carry):
            @pl.when(jnp.logical_and(native(orb, m) == orb, line_of(m) != aux))
            def _():
                forward(m).wait_send()

            return carry

        lax.fori_loop(0, groups, passed, 0)


def pair_totals(integrals, coeffs, domains):
    n_aux, n_orb = lax.axis_size("aux"), lax.axis_size("orb")
    occupied, aux_rows, ao_local = integrals.shape
    groups = occupied // 2
    half = aux_rows // 2
    per_group = half // CHUNK_ROWS
    chunks = groups * per_group
    row_groups = occupied // n_aux // 2
    assert groups == n_orb and half % CHUNK_ROWS == 0
    parts = next(n for n in (4, 2, 1) if per_group % n == 0)
    vir_blocks = coeffs.shape[1] // BS
    dims = (n_aux, n_orb, groups, per_group, row_groups, parts)
    bf16 = jnp.bfloat16
    vmem = pltpu.VMEM
    dma = pltpu.SemaphoreType.DMA
    return pl.pallas_call(
        functools.partial(exchange, dims),
        out_shape=jax.ShapeDtypeStruct((row_groups, GROUP, GROUP), jnp.float32),
        in_specs=[
            pl.BlockSpec(memory_space=pltpu.SMEM),
            pl.BlockSpec(memory_space=pl.ANY),
            pl.BlockSpec(memory_space=pl.ANY),
        ],
        out_specs=pl.BlockSpec(memory_space=pltpu.VMEM),
        scratch_shapes=[
            vmem((vir_blocks, ao_local, BS), bf16),
            vmem((groups, GROUP, GROUP), jnp.float32),
            vmem((SLOTS, 2, CHUNK_ROWS, ao_local), bf16),
            vmem((OTHER_SLOTS, 2, CHUNK_ROWS, ao_local), bf16),
            vmem((chunks, CHUNK_ROWS, GROUP), bf16),
            vmem((chunks, CHUNK_ROWS, GROUP), bf16),
            vmem((min(SEND_SLOTS, chunks), CHUNK_ROWS, GROUP), bf16),
            vmem((groups, parts, GROUP, half // parts), bf16),
            vmem((2, groups, GROUP, GROUP), bf16),
            vmem((n_aux - 1, row_groups, groups, GROUP, GROUP), bf16),
            vmem((row_groups, groups, GROUP, GROUP), bf16),
            vmem((row_groups, groups, GROUP, GROUP), bf16),
            vmem((2, row_groups, GROUP, GROUP), bf16),
            vmem((2, groups, GROUP, GROUP), bf16),
            vmem((row_groups, GROUP, GROUP), bf16),
            dma((vir_blocks,)),
            dma((SLOTS,)),
            dma((OTHER_SLOTS,)),
            dma((min(SEND_SLOTS, chunks),)),
            dma((chunks,)),
            dma((chunks,)),
            dma((chunks,)),
            dma((2, groups)),
            dma((n_aux - 1, row_groups, groups)),
            dma((row_groups, groups)),
            dma((2, row_groups)),
            dma((row_groups, groups)),
            dma((2, groups)),
            dma((groups,)),
            dma((row_groups,)),
        ],
        compiler_params=pltpu.CompilerParams(
            collective_id=0, has_side_effects=True, vmem_limit_bytes=63 * 1024 * 1024
        ),
        cost_estimate=pl.CostEstimate(
            flops=2 * occupied * aux_rows * ao_local * BS, bytes_accessed=2 * integrals.size, transcendentals=0
        ),
    )(domains, coeffs, integrals)


def shards(integrals, coeffs, domains, eps_occ, eps_vir, pair_mask):
    occupied = integrals.shape[0]
    vir_blocks = coeffs.shape[1] // BS
    own_count = occupied // lax.axis_size("orb")
    row_count = occupied // lax.axis_size("aux")
    aux_index = lax.axis_index("aux")
    orb_index = lax.axis_index("orb")
    totals = pair_totals(integrals, coeffs, domains).reshape(row_count, BS, own_count, BS)
    pair_ints = totals * (1.0 / jnp.sqrt(jnp.float32(NAUX)))
    selector = domains[:, None] == jnp.arange(vir_blocks, dtype=jnp.int32)[None, :]
    vir_energy = jnp.dot(
        selector.astype(jnp.float32),
        eps_vir.reshape(vir_blocks, BS),
        precision=lax.Precision.HIGHEST,
    )
    vir_rows = lax.dynamic_slice_in_dim(vir_energy, aux_index * row_count, row_count, 0)
    vir_cols = lax.dynamic_slice_in_dim(vir_energy, orb_index * own_count, own_count, 0)
    occ_rows = lax.dynamic_slice_in_dim(eps_occ, aux_index * row_count, row_count, 0)
    occ_cols = lax.dynamic_slice_in_dim(eps_occ, orb_index * own_count, own_count, 0)
    denominator = (
        vir_rows[:, :, None, None]
        + vir_cols[None, None, :, :]
        - occ_rows[:, None, None, None]
        - occ_cols[None, None, :, None]
    )
    screen = pair_mask.astype(jnp.float32)
    amplitudes = screen[:, None, :, None] * pair_ints / denominator
    energies = -jnp.sum(pair_ints * amplitudes, axis=(1, 3)) / float(BS * BS)
    return (amplitudes.astype(jnp.bfloat16), energies)


def solution(mesh):
    return jax.shard_map(
        shards,
        mesh=mesh,
        in_specs=(P(None, "aux", "orb"), P("orb", None), P(), P(), P(), P("aux", "orb")),
        out_specs=(P("aux", None, "orb", None), P("aux", "orb")),
        check_vma=False,
    )
```
